128 devices in a mesh: pat: 16 (over x, y), tile: 8 (over z, core).
Axes of the slice: x: 4, y: 4, z: 4, core: 2. Of those that a mesh axis runs over, the one named last changes fastest.
Arguments:
- scanned: int32 [32, 32], P('tile', 'pat'), may hold values from 0 to 1, as said below
- measured: float32 [32, 32, 256, 256], P('tile', 'pat'), may hold values from 0 to 2
- obj: float32 [2, 2, 4096, 4096], P(None, None, 'tile', 'pat'), may hold values from -5 to 5
- probe: float32 [2, 256, 256], replicated, may hold values from -6 to 6
Outputs:
- grad_obj: float32 [2, 2, 4096, 4096], P(None, None, 'tile', 'pat')
- grad_probe: float32 [2, 256, 256], replicated
The draws below stay inside these ranges and needn't reach their ends.
Inputs may be any that keep to these rules, and one draw needn't show every extreme that they name: `scanned`: the grid points of rows 0 to 3 and columns 0 to 1 are all 1; the last grid row and the last grid column are all 0; the share of 1 may differ between groups of four grid rows.
All inputs are finite; a program needn't handle non-finite values.
Results may differ from the reference program's by a relative error of at most 0.0003.
Values sent between devices are 32-bit elements; how exact they have to be, the bound alone decides.
A program may use at most 128 MiB of HBM per device.

```python
import jax
import jax.numpy as jnp
from jax import lax

W = 256
SLICES = 2
OBJ_R = 4096
OBJ_C = 4096
GRID_R = 32
GRID_C = 32


def draw_scanned(key, part):
    key = jax.random.fold_in(key, 17)
    block_rows = GRID_R // 4
    levels = jax.random.randint(jax.random.fold_in(key, 1), (block_rows, 1), 1, 11)
    levels = jnp.repeat(levels, 4, axis=0)
    rolls = jax.random.randint(jax.random.fold_in(key, 2), (GRID_R, GRID_C), 0, 10)
    live = (rolls < levels).astype(jnp.int32)
    rows = jnp.arange(GRID_R)[:, None]
    cols = jnp.arange(GRID_C)[None, :]
    live = jnp.where((rows < 4) & (cols < 2), 1, live)
    live = jnp.where((rows == GRID_R - 1) | (cols == GRID_C - 1), 0, live)
    return live.astype(jnp.int32)


def steps_of(own_key, dims, split, low, top_value):
    def one(dim, parts):
        heights = jax.random.uniform(jax.random.fold_in(jax.random.fold_in(own_key, 6), dim), (parts,), jnp.float32, low / len(split), top_value / len(split))
        return jnp.repeat(jnp.exp(heights), dims[dim] // parts).reshape((-1,) + (1,) * (len(dims) - dim - 1))

    factor_of = one(*split[0])
    for cut in split[1:]:
        factor_of = factor_of * one(*cut)
    return factor_of


def centred(rng, shape, scale, bound, cuts=(), kind=jnp.bfloat16):
    level = steps_of(rng, shape, cuts, -0.22, 0.18) if cuts else 1.0
    drawn = jax.random.normal(rng, shape, jnp.float32) * scale * level
    return jnp.minimum(jnp.maximum(drawn, -bound), bound).astype(kind)


def setup_inputs(seed: int = 0) -> dict:
    keys = jax.random.split(jax.random.key(seed), 5)
    scanned = draw_scanned(jax.random.fold_in(keys[4], 71), 0)
    measured = jnp.clip(2.0 * jax.random.uniform(keys[1], (GRID_R, GRID_C, W, W), jnp.float32) ** steps_of(keys[1], (GRID_R, GRID_C, W, W), ((0, 8), (1, 16)), -0.2, 0.2), 0.0, 2.0)
    obj = centred(keys[2], (SLICES, 2, OBJ_R, OBJ_C), 0.7, 5.0, ((2, 8), (3, 16)), jnp.float32)
    probe = centred(keys[3], (2, W, W), 1.0, 6.0, (), jnp.float32)
    return {"scanned": scanned, "measured": measured, "obj": obj, "probe": probe}


PHASE_SCALE = 40.0

def propagator(size):
    index = jnp.arange(size, dtype=jnp.int32)
    signed = jnp.where(index < (size + 1) // 2, index, index - size).astype(jnp.float32) / size
    phase = PHASE_SCALE * (signed[:, None] ** 2 + signed[None, :] ** 2)
    return (jnp.cos(phase), -jnp.sin(phase))

def pattern_loss(window, probe, measured):
    size = probe.shape[-1]
    prop_re, prop_im = propagator(size)
    spread = lax.complex(prop_re, prop_im)
    wave = lax.complex(probe[0], probe[1]) * lax.complex(window[0, 0], window[0, 1])
    for layer in range(1, window.shape[0]):
        moved = jnp.fft.ifft2(jnp.fft.fft2(wave, norm='ortho') * spread, norm='ortho')
        wave = moved * lax.complex(window[layer, 0], window[layer, 1])
    far = jnp.fft.fft2(wave, norm='ortho')
    diff = jnp.real(far) ** 2 + jnp.imag(far) ** 2 - measured
    return 0.5 * jnp.sum(diff * diff)

def reference(scanned, measured, obj, probe):
    size = probe.shape[-1]
    step = size // 2
    grid_r, grid_c = scanned.shape
    padded = jnp.pad(obj, ((0, 0), (0, 0), (0, size), (0, size)))
    zero = jnp.zeros((), jnp.int32)
    slices = obj.shape[0]

    def visit(carry, index):
        grad_pad, grad_probe = carry
        row = (index // grid_c).astype(jnp.int32)
        col = (index % grid_c).astype(jnp.int32)
        starts = (zero, zero, (row * step).astype(jnp.int32), (col * step).astype(jnp.int32))
        window = lax.dynamic_slice(padded, starts, (slices, 2, size, size))
        g_win, g_probe = jax.grad(pattern_loss, argnums=(0, 1))(window, probe, measured[row, col])
        weight = scanned[row, col].astype(jnp.float32)
        current = lax.dynamic_slice(grad_pad, starts, (slices, 2, size, size))
        grad_pad = lax.dynamic_update_slice(grad_pad, current + weight * g_win, starts)
        return ((grad_pad, grad_probe + weight * g_probe), None)
    init = (jnp.zeros(padded.shape, jnp.float32), jnp.zeros(probe.shape, jnp.float32))
    (grad_pad, grad_probe), _ = lax.scan(visit, init, jnp.arange(grid_r * grid_c, dtype=jnp.int32))
    return (grad_pad[:, :, :obj.shape[2], :obj.shape[3]], grad_probe)
```

```python
import functools

import jax
import jax.numpy as jnp
import ml_dtypes
import numpy as np
from jax import lax
from jax.experimental import pallas as pl
from jax.experimental.pallas import tpu as pltpu
from jax.sharding import PartitionSpec as P

SIDE, HALF = 256, 128
PHASE_SCALE = 40.0

def embed(m):
    return np.block([[m.real, m.imag], [-m.imag, m.real]])

def tables():
    n = np.arange(SIDE)
    dft = np.exp(-2j * np.pi * (n[:, None] * n[None, :] % SIDE) / SIDE) / 16.0
    signed = np.where(n < HALF, n, n - SIDE) / SIDE
    spread = np.exp(-1j * PHASE_SCALE * signed**2)
    move = np.conj(dft) @ (spread[:, None] * dft)
    near, across = move[:HALF, :HALF], move[:HALF, HALF:]
    ce, co = (near + across) / 2, (near - across) / 2
    a, b = dft[:HALF, 0::2], dft[:HALF, 1::2]
    right = [embed(ce), embed(co), embed(a), embed(b), embed(b.T)]
    full = np.stack(right + [m.T for m in right])
    hi = full.astype(ml_dtypes.bfloat16)
    lo = (full - hi.astype(np.float64)).astype(ml_dtypes.bfloat16)
    order = np.concatenate([np.arange(0, SIDE, 2), np.arange(1, SIDE, 2)])
    perm = np.zeros((SIDE, SIDE))
    perm[order, n] = 1.0
    return np.concatenate([hi, lo, perm[None].astype(ml_dtypes.bfloat16)])

CE, CO, FA, FB, FBT = range(5)
LEFT = 5
LOW = 10
PERM = 20

def split(x):
    hi = x.astype(jnp.bfloat16)
    return hi, (x - hi.astype(jnp.float32)).astype(jnp.bfloat16)

def dot(l, r):
    return jnp.dot(l, r, preferred_element_type=jnp.float32)

def mul_right(x, tab, k):
    hi, lo = split(x)
    wh, wl = tab[k], tab[k + LOW]
    return dot(hi, wh) + dot(lo, wh) + dot(hi, wl)

def mul_left(x, tab, k):
    hi, lo = split(x)
    wh, wl = tab[k + LEFT], tab[k + LEFT + LOW]
    return dot(wh, hi) + dot(wl, hi) + dot(wh, lo)

def lanes(re, im):
    rl, rr, il, ir = re[:, :HALF], re[:, HALF:], im[:, :HALF], im[:, HALF:]
    cat = lambda p, q: jnp.concatenate([p, q], axis=1)
    return cat(rl + rr, il + ir), cat(rl - rr, il - ir)

def rows(re, im):
    rt, rb, it, ib = re[:HALF], re[HALF:], im[:HALF], im[HALF:]
    cat = lambda p, q: jnp.concatenate([p, q], axis=0)
    return cat(rt + rb, it + ib), cat(rt - rb, it - ib)

def planes_of_lanes(even, odd):
    re = jnp.concatenate([even[:, :HALF], odd[:, :HALF]], axis=1)
    im = jnp.concatenate([even[:, HALF:], odd[:, HALF:]], axis=1)
    return re, im

def planes_of_rows(even, odd):
    re = jnp.concatenate([even[:HALF], odd[:HALF]], axis=0)
    im = jnp.concatenate([even[HALF:], odd[HALF:]], axis=0)
    return re, im

def spread(re, im, tab):
    e, o = lanes(re, im)
    e, o = mul_right(e, tab, CE), mul_right(o, tab, CO)
    yield
    re, im = planes_of_lanes(e, o)
    e, o = rows(re, im)
    e, o = mul_left(e, tab, CE), mul_left(o, tab, CO)
    yield
    re, im = planes_of_rows(e + o, e - o)
    l = lambda t: jnp.concatenate([t[:, :HALF] + t[:, HALF:], t[:, :HALF] - t[:, HALF:]], axis=1)
    return l(re), l(im)

def to_far(re, im, tab):
    e, o = lanes(re, im)
    e, o = mul_right(e, tab, FA), mul_right(o, tab, FB)
    yield
    re, im = planes_of_lanes(e, o)
    e, o = rows(re, im)
    e, o = mul_left(e, tab, FA), mul_left(o, tab, FB)
    yield
    return e, o

def from_far(even, odd, tab):
    e, o = mul_left(even, tab, FA), mul_left(odd, tab, FBT)
    yield
    re, im = planes_of_rows(e + o, e - o)
    e = jnp.concatenate([re[:, :HALF], im[:, :HALF]], axis=1)
    o = jnp.concatenate([re[:, HALF:], im[:, HALF:]], axis=1)
    e, o = mul_right(e, tab, FA), mul_right(o, tab, FBT)
    yield
    return planes_of_lanes(e + o, e - o)

def point(weight, pad, grad, meas, probe, pgrad, tab, order, a, b):
    r = pl.ds(pl.multiple_of(a * HALF, HALF), SIDE)
    c = pl.ds(pl.multiple_of(b * HALF, HALF), SIDE)
    pr, pi = probe[0], probe[1]
    o0r, o0i = pad[0, 0, r, c], pad[0, 1, r, c]
    ur, ui = yield from spread(pr * o0r - pi * o0i, pr * o0i + pi * o0r, tab)
    o1r, o1i = pad[1, 0, r, c], pad[1, 1, r, c]
    even, odd = yield from to_far(ur * o1r - ui * o1i, ur * o1i + ui * o1r, tab)
    hi, lo = split(meas[a, b])
    m = dot(hi, tab[PERM]) + dot(lo, tab[PERM])
    order[0], order[1] = m[:, :HALF], m[:, HALF:]

    def pull(f, start):
        pick = pl.ds(start, HALF, stride=2)
        m = jnp.concatenate([order[0, pick, :], order[1, pick, :]], axis=1)
        fr, fi = f[:HALF], f[HALF:]
        d = (fr * fr + fi * fi - m) * (2.0 * weight)
        return jnp.concatenate([d * fr, -(d * fi)], axis=0)

    gr, gi = yield from from_far(pull(even, 0), pull(odd, 1), tab)
    grad[1, 0, r, c] += ur * gr - ui * gi
    grad[1, 1, r, c] -= ur * gi + ui * gr
    o1r, o1i = pad[1, 0, r, c], pad[1, 1, r, c]
    gr, gi = yield from spread(o1r * gr - o1i * gi, o1r * gi + o1i * gr, tab)
    pr, pi = probe[0], probe[1]
    grad[0, 0, r, c] += pr * gr - pi * gi
    grad[0, 1, r, c] -= pr * gi + pi * gr
    o0r, o0i = pad[0, 0, r, c], pad[0, 1, r, c]
    pgrad[0:SIDE] += o0r * gr - o0i * gi
    pgrad[SIDE:] -= o0r * gi + o0i * gr


def run(work):
    work = list(work)
    while work:
        for w in list(work):
            if next(w, work) is work:
                work.remove(w)


MESH = pl.DeviceIdType.MESH


def kernel(tiles, pats, scanned, obj, meas_in, probe_in, tab_in, out_obj, out_probe,
           pad, grad, meas, probe, tab, order, pgrad, from_left, from_up, part1, part2, share, total,
           local_sem, halo_send, halo_recv, grad_send, grad_recv, sum_send, sum_recv):
    tile, pat = lax.axis_index("tile"), lax.axis_index("pat")
    left, right = {"pat": lax.rem(pat + pats - 1, pats)}, {"pat": lax.rem(pat + 1, pats)}
    up, down = {"tile": lax.rem(tile + tiles - 1, tiles)}, {"tile": lax.rem(tile + 1, tiles)}

    def remote(src, dst, send, recv, k, device):
        return pltpu.make_async_remote_copy(
            src_ref=src, dst_ref=dst, send_sem=send.at[k], recv_sem=recv.at[k],
            device_id=device, device_id_type=MESH)

    loads = [
        pltpu.make_async_copy(obj, pad.at[:, :, pl.ds(0, 512), pl.ds(0, 256)], local_sem.at[0]),
        pltpu.make_async_copy(probe_in, probe, local_sem.at[1]),
        pltpu.make_async_copy(tab_in, tab, local_sem.at[2]),
        pltpu.make_async_copy(meas_in, meas, local_sem.at[3]),
    ]
    for copy in loads:
        copy.start()

    barrier = pltpu.get_barrier_semaphore()
    for o in range(1, tiles):
        pl.semaphore_signal(barrier, inc=1, device_id={"tile": lax.rem(tile + o, tiles)}, device_id_type=MESH)
    for o in range(1, pats):
        pl.semaphore_signal(barrier, inc=1, device_id={"pat": lax.rem(pat + o, pats)}, device_id_type=MESH)
    grad[...] = jnp.zeros_like(grad)
    pgrad[...] = jnp.zeros_like(pgrad)
    pl.semaphore_wait(barrier, tiles - 1 + pats - 1)

    first, second = pl.ds(0, HALF), pl.ds(256, HALF)
    chunk = [pl.ds(k * HALF, HALF) for k in range(5)]
    beside = [
        remote(obj.at[:, :, chunk[k], first], pad.at[:, :, chunk[k], second], halo_send, halo_recv, k, left)
        for k in range(4)
    ]
    below = remote(obj.at[:, :, chunk[0], :], pad.at[:, :, chunk[4], pl.ds(0, 256)], halo_send, halo_recv, 4, up)
    corner = remote(pad.at[:, :, chunk[0], second], pad.at[:, :, chunk[4], second], halo_send, halo_recv, 5, up)
    for k in (3, 0, 1, 2):
        beside[k].start()
    below.start()
    for copy in loads:
        copy.wait()

    low = remote(grad.at[:, :, chunk[4], :], from_up, grad_send, grad_recv, 4, down)
    out = [
        remote(grad.at[:, :, chunk[k], second], from_left.at[:, :, chunk[k], :], grad_send, grad_recv, k, right)
        for k in range(4)
    ]

    def step(i, _):
        @pl.when(i == 1)
        def _():
            below.wait()

        @pl.when(i == 2)
        def _():
            beside[3].wait()
            beside[0].wait()
            corner.start()
            beside[1].wait()
            corner.wait()

        @pl.when(i == 3)
        def _():
            low.start()
            beside[2].wait()

        ahead = i < 2
        b = i // 2
        a0 = jnp.where(ahead, 2 * i, 7 - 2 * i)
        a1 = jnp.where(ahead, 2 * i + 1, 2 * i - 4)
        run(
            point(scanned[a, b].astype(jnp.float32), pad, grad, meas, probe, pgrad, tab, order.at[k], a, b)
            for k, a in enumerate((a0, a1))
        )
        return 0

    lax.fori_loop(0, 4, step, 0)

    rows_of = lambda t: pl.ds(pl.multiple_of(t * 64, 64), 64)
    cell = lambda p: (pl.ds(pl.multiple_of((p // 2) * 8, 8), 8), pl.ds(pl.multiple_of((p % 2) * HALF, HALF), HALF))
    flat = pgrad
    sums1, sums2, spread2, spread1 = [], [], [], []
    for o in range(1, tiles):
        t = lax.rem(tile + o, tiles)
        sums1.append(remote(flat.at[rows_of(t), :], part1.at[o - 1], sum_send, sum_recv, o - 1, {"tile": t}))
    for copy in sums1:
        copy.start()

    for k in (1, 2, 3):
        out[k].start()
    low.wait()
    grad[:, :, 0:HALF, :] += from_up[...]
    out[0].start()

    for copy in sums1:
        copy.wait()
    acc = flat[rows_of(tile), :]
    for k in range(tiles - 1):
        acc = acc + part1[k]
    share[...] = acc
    for o in range(1, pats):
        p = lax.rem(pat + o, pats)
        sums2.append(remote(share.at[cell(p)], part2.at[o - 1], sum_send, sum_recv, 7 + o - 1, {"pat": p}))
    for copy in sums2:
        copy.start()
    for copy in sums2:
        copy.wait()
    acc = share[cell(pat)]
    for k in range(pats - 1):
        acc = acc + part2[k]
    mine = total.at[rows_of(tile), :]
    total_cell = mine.at[cell(pat)]
    total_cell[...] = acc
    for o in range(1, pats):
        p = lax.rem(pat + o, pats)
        spread2.append(remote(total_cell, total_cell, sum_send, sum_recv, 22 + o - 1, {"pat": p}))
    for copy in spread2:
        copy.start()
    for copy in spread2:
        copy.wait()
    for o in range(1, tiles):
        t = lax.rem(tile + o, tiles)
        spread1.append(remote(mine, mine, sum_send, sum_recv, 37 + o - 1, {"tile": t}))
    for copy in spread1:
        copy.start()

    stores = []
    for n, k in enumerate((1, 2, 3, 0)):
        out[k].wait()
        grad[:, :, chunk[k], 0:HALF] += from_left[:, :, chunk[k], :]
        store = pltpu.make_async_copy(
            grad.at[:, :, chunk[k], pl.ds(0, 256)], out_obj.at[:, :, chunk[k], :], local_sem.at[4 + n])
        store.start()
        stores.append(store)
    for copy in spread1:
        copy.wait()
    last = pltpu.make_async_copy(total, out_probe, local_sem.at[8])
    last.start()
    for copy in stores:
        copy.wait()
    last.wait()


def on_device(scanned, measured, obj, probe):
    tiles, pats = lax.axis_size("tile"), lax.axis_size("pat")
    table = jnp.asarray(tables())
    anywhere = pl.BlockSpec(memory_space=pl.ANY)
    f32 = jnp.float32
    vmem = lambda *shape: pltpu.VMEM(shape, f32)
    dma = lambda n: pltpu.SemaphoreType.DMA((n,))
    sums = 2 * (tiles - 1 + pats - 1)
    grad_obj, grad_probe = pl.pallas_call(
        functools.partial(kernel, tiles, pats),
        out_shape=[jax.ShapeDtypeStruct(obj.shape, f32), jax.ShapeDtypeStruct((2 * SIDE, SIDE), f32)],
        in_specs=[pl.BlockSpec(memory_space=pltpu.SMEM)] + [anywhere] * 4,
        out_specs=[anywhere, anywhere],
        scratch_shapes=[
            vmem(2, 2, 640, 384), vmem(2, 2, 640, 384), vmem(4, 2, SIDE, SIDE), vmem(2, SIDE, SIDE),
            pltpu.VMEM(table.shape, jnp.bfloat16), vmem(2, 2, SIDE, HALF), vmem(2 * SIDE, SIDE),
            vmem(2, 2, 512, HALF), vmem(2, 2, HALF, 384),
            vmem(tiles - 1, 64, SIDE), vmem(pats - 1, 8, HALF), vmem(64, SIDE), vmem(2 * SIDE, SIDE),
            dma(9), dma(6), dma(6), dma(5), dma(5), dma(sums), dma(sums),
        ],
        compiler_params=pltpu.CompilerParams(
            collective_id=0, has_side_effects=True, vmem_limit_bytes=56 * 2**20),
        cost_estimate=pl.CostEstimate(flops=27 * 10**9, bytes_accessed=10 * 2**20, transcendentals=0),
    )(scanned, obj, measured, probe, table)
    return grad_obj, grad_probe.reshape(probe.shape)


def solution(mesh):
    in_specs = (P("tile", "pat"), P("tile", "pat", None, None), P(None, None, "tile", "pat"), P())
    out_specs = (P(None, None, "tile", "pat"), P())
    return jax.shard_map(
        on_device, mesh=mesh, in_specs=in_specs, out_specs=out_specs, check_vma=False
    )
```

```python
import functools

import jax
import jax.numpy as jnp
import ml_dtypes
import numpy as np
from jax import lax
from jax.experimental import pallas as pl
from jax.experimental.pallas import tpu as pltpu
from jax.sharding import PartitionSpec as P

SIDE, HALF = 256, 128
PHASE_SCALE = 40.0

def embed(m):
    return np.block([[m.real, m.imag], [-m.imag, m.real]])

def tables():
    n = np.arange(SIDE)
    dft = np.exp(-2j * np.pi * (n[:, None] * n[None, :] % SIDE) / SIDE) / 16.0
    signed = np.where(n < HALF, n, n - SIDE) / SIDE
    spread = np.exp(-1j * PHASE_SCALE * signed**2)
    move = np.conj(dft) @ (spread[:, None] * dft)
    near, across = move[:HALF, :HALF], move[:HALF, HALF:]
    ce, co = (near + across) / 2, (near - across) / 2
    a, b = dft[:HALF, 0::2], dft[:HALF, 1::2]
    right = [embed(ce), embed(co), embed(a), embed(b), embed(b.T)]
    full = np.stack(right + [m.T for m in right])
    hi = full.astype(ml_dtypes.bfloat16)
    lo = (full - hi.astype(np.float64)).astype(ml_dtypes.bfloat16)
    order = np.concatenate([np.arange(0, SIDE, 2), np.arange(1, SIDE, 2)])
    perm = np.zeros((SIDE, SIDE))
    perm[order, n] = 1.0
    return np.concatenate([hi, lo, perm[None].astype(ml_dtypes.bfloat16)])

CE, CO, FA, FB, FBT = range(5)
LEFT = 5
LOW = 10
PERM = 20

def split(x):
    hi = x.astype(jnp.bfloat16)
    return hi, (x - hi.astype(jnp.float32)).astype(jnp.bfloat16)

def dot(l, r):
    return jnp.dot(l, r, preferred_element_type=jnp.float32)

def mul_right(x, tab, k):
    hi, lo = split(x)
    wh, wl = tab[k], tab[k + LOW]
    return dot(hi, wh) + dot(lo, wh) + dot(hi, wl)

def mul_left(x, tab, k):
    hi, lo = split(x)
    wh, wl = tab[k + LEFT], tab[k + LEFT + LOW]
    return dot(wh, hi) + dot(wl, hi) + dot(wh, lo)

def lanes(re, im):
    rl, rr, il, ir = re[:, :HALF], re[:, HALF:], im[:, :HALF], im[:, HALF:]
    cat = lambda p, q: jnp.concatenate([p, q], axis=1)
    return cat(rl + rr, il + ir), cat(rl - rr, il - ir)

def rows(re, im):
    rt, rb, it, ib = re[:HALF], re[HALF:], im[:HALF], im[HALF:]
    cat = lambda p, q: jnp.concatenate([p, q], axis=0)
    return cat(rt + rb, it + ib), cat(rt - rb, it - ib)

def planes_of_lanes(even, odd):
    re = jnp.concatenate([even[:, :HALF], odd[:, :HALF]], axis=1)
    im = jnp.concatenate([even[:, HALF:], odd[:, HALF:]], axis=1)
    return re, im

def planes_of_rows(even, odd):
    re = jnp.concatenate([even[:HALF], odd[:HALF]], axis=0)
    im = jnp.concatenate([even[HALF:], odd[HALF:]], axis=0)
    return re, im

def spread(re, im, tab):
    e, o = lanes(re, im)
    e, o = mul_right(e, tab, CE), mul_right(o, tab, CO)
    yield
    re, im = planes_of_lanes(e, o)
    e, o = rows(re, im)
    e, o = mul_left(e, tab, CE), mul_left(o, tab, CO)
    yield
    re, im = planes_of_rows(e + o, e - o)
    l = lambda t: jnp.concatenate([t[:, :HALF] + t[:, HALF:], t[:, :HALF] - t[:, HALF:]], axis=1)
    return l(re), l(im)

def to_far(re, im, tab):
    e, o = lanes(re, im)
    e, o = mul_right(e, tab, FA), mul_right(o, tab, FB)
    yield
    re, im = planes_of_lanes(e, o)
    e, o = rows(re, im)
    e, o = mul_left(e, tab, FA), mul_left(o, tab, FB)
    yield
    return e, o

def from_far(even, odd, tab):
    e, o = mul_left(even, tab, FA), mul_left(odd, tab, FBT)
    yield
    re, im = planes_of_rows(e + o, e - o)
    e = jnp.concatenate([re[:, :HALF], im[:, :HALF]], axis=1)
    o = jnp.concatenate([re[:, HALF:], im[:, HALF:]], axis=1)
    e, o = mul_right(e, tab, FA), mul_right(o, tab, FBT)
    yield
    return planes_of_lanes(e + o, e - o)

def point(scanned, pad, grad, meas, probe, pgrad, tab, order, a, b):
    r = pl.ds(pl.multiple_of(a * HALF, HALF), SIDE)
    c = pl.ds(pl.multiple_of(b * HALF, HALF), SIDE)
    here = [lax.broadcasted_iota(jnp.int32, scanned.shape, n) == v for n, v in enumerate((a, b))]
    live = jnp.where(here[0] & here[1], scanned[...].astype(jnp.float32), 0.0)
    weight = jnp.sum(jnp.sum(live, axis=1, keepdims=True), axis=0, keepdims=True)
    pr, pi = probe[0], probe[1]
    o0r, o0i = pad[0, 0, r, c], pad[0, 1, r, c]
    ur, ui = yield from spread(pr * o0r - pi * o0i, pr * o0i + pi * o0r, tab)
    o1r, o1i = pad[1, 0, r, c], pad[1, 1, r, c]
    even, odd = yield from to_far(ur * o1r - ui * o1i, ur * o1i + ui * o1r, tab)
    hi, lo = split(meas[a, b])
    m = dot(hi, tab[PERM]) + dot(lo, tab[PERM])
    order[0], order[1] = m[:, :HALF], m[:, HALF:]

    def pull(f, start):
        pick = pl.ds(start, HALF, stride=2)
        m = jnp.concatenate([order[0, pick, :], order[1, pick, :]], axis=1)
        fr, fi = f[:HALF], f[HALF:]
        d = (fr * fr + fi * fi - m) * (2.0 * weight)
        return jnp.concatenate([d * fr, -(d * fi)], axis=0)

    gr, gi = yield from from_far(pull(even, 0), pull(odd, 1), tab)
    grad[1, 0, r, c] += ur * gr - ui * gi
    grad[1, 1, r, c] -= ur * gi + ui * gr
    o1r, o1i = pad[1, 0, r, c], pad[1, 1, r, c]
    gr, gi = yield from spread(o1r * gr - o1i * gi, o1r * gi + o1i * gr, tab)
    pr, pi = probe[0], probe[1]
    grad[0, 0, r, c] += pr * gr - pi * gi
    grad[0, 1, r, c] -= pr * gi + pi * gr
    o0r, o0i = pad[0, 0, r, c], pad[0, 1, r, c]
    pgrad[0:SIDE] += o0r * gr - o0i * gi
    pgrad[SIDE:] -= o0r * gi + o0i * gr


def run(work):
    work = list(work)
    while work:
        for w in list(work):
            if next(w, work) is work:
                work.remove(w)


MESH = pl.DeviceIdType.MESH


def kernel(tiles, pats, scanned_in, obj, meas_in, probe_in, tab_in, out_obj, out_probe,
           scanned, pad, grad, meas, probe, tab, order, pgrad, from_left, from_up, half, part, total,
           local_sem, halo_send, halo_recv, grad_send, grad_recv, sum_send, sum_recv, inside):
    tile, pat = lax.axis_index("tile"), lax.axis_index("pat")
    left, right = {"pat": lax.rem(pat + pats - 1, pats)}, {"pat": lax.rem(pat + 1, pats)}
    up, down = {"tile": lax.rem(tile + tiles - 1, tiles)}, {"tile": lax.rem(tile + 1, tiles)}

    def remote(src, dst, send, recv, k, device):
        return pltpu.make_async_remote_copy(
            src_ref=src, dst_ref=dst, send_sem=send.at[k], recv_sem=recv.at[k],
            device_id=device, device_id_type=MESH)

    loads = [
        pltpu.make_async_copy(obj, pad.at[:, :, pl.ds(0, 512), pl.ds(0, 256)], local_sem.at[0]),
        pltpu.make_async_copy(probe_in, probe, local_sem.at[1]),
        pltpu.make_async_copy(tab_in, tab, local_sem.at[2]),
        pltpu.make_async_copy(meas_in, meas, local_sem.at[3]),
        pltpu.make_async_copy(scanned_in, scanned, local_sem.at[9]),
    ]
    for copy in loads:
        copy.start()

    barrier = pltpu.get_barrier_semaphore()
    for o in range(1, tiles):
        pl.semaphore_signal(barrier, inc=1, device_id={"tile": lax.rem(tile + o, tiles)}, device_id_type=MESH)
    for o in range(1, pats):
        pl.semaphore_signal(barrier, inc=1, device_id={"pat": lax.rem(pat + o, pats)}, device_id_type=MESH)
    grad[...] = jnp.zeros_like(grad)
    pgrad[...] = jnp.zeros_like(pgrad)
    pl.semaphore_wait(barrier, tiles - 1 + pats - 1)

    first, second = pl.ds(0, HALF), pl.ds(256, HALF)
    chunk = [pl.ds(k * HALF, HALF) for k in range(5)]
    piece = [pl.ds(k * 64, 64) for k in range(8)]
    beside = [
        remote(obj.at[:, :, piece[k], first], pad.at[:, :, piece[k], second], halo_send, halo_recv, k, left)
        for k in range(8)
    ]
    below = remote(obj.at[:, :, chunk[0], :], pad.at[:, :, chunk[4], pl.ds(0, 256)], halo_send, halo_recv, 8, up)
    corner = remote(pad.at[:, :, chunk[0], second], pad.at[:, :, chunk[4], second], halo_send, halo_recv, 9, up)
    core = lax.rem(tile, 2)

    @pl.when(core == 0)
    def _():
        for k in range(8):
            beside[k].start()

    below.start()
    for copy in loads:
        copy.wait()

    low_first = remote(
        grad.at[:, :, chunk[4], first], from_up.at[:, :, :, first], grad_send, grad_recv, 6, down)
    low = remote(
        grad.at[:, :, chunk[4], chunk[1]], from_up.at[:, :, :, chunk[1]], grad_send, grad_recv, 4, down)
    low_corner = remote(
        grad.at[:, :, chunk[4], second], from_up.at[:, :, :, second], grad_send, grad_recv, 5, down)
    out = [
        remote(grad.at[:, :, chunk[k], second], from_left.at[:, :, chunk[k], :], grad_send, grad_recv, k, right)
        for k in range(4)
    ]

    def add_corner():
        grad[:, :, 0:HALF, 256:] += from_up[:, :, :, 256:]
        out[0].start()

    def step(i, _):
        @pl.when(i == 1)
        def _():
            below.wait()

        @pl.when(i == 2)
        def _():
            @pl.when(core == 1)
            def _():
                for k in range(3):
                    beside[k].start()

            for o in range(1, pats):
                pl.semaphore_signal(inside, inc=1, device_id={"pat": lax.rem(pat + o, pats)}, device_id_type=MESH)
            low_first.start()
            for k in range(5):
                beside[k].wait_send()
                pl.when(core == 1)(beside[k + 3].start)
                if k == 2:
                    beside[0].wait_recv()
                    beside[1].wait_recv()
                    corner.start()
            for k in range(2, 6):
                beside[k].wait_recv()

        @pl.when(i == 3)
        def _():
            out[1].start()

            @pl.when(core == 1)
            def _():
                low_corner.wait_recv()
                add_corner()

            for k in range(5, 8):
                beside[k].wait_send()
            beside[6].wait_recv()
            beside[7].wait_recv()
            corner.wait()

        b = i // 2
        a = 2 * i - 4 * b
        run(
            point(scanned, pad, grad, meas, probe, pgrad, tab, order.at[k], a + k, b)
            for k in range(2)
        )
        return 0

    lax.fori_loop(0, 4, step, 0)

    other = {"tile": tile + 1 - 2 * core}
    layer, side_x, side_y = tile // 2, pat // 4, lax.rem(pat, 4)
    half_of = lambda c: pl.ds(pl.multiple_of(c * 256, 256), 256)
    trips = [(x, y, z) for x in range(4) for y in range(4) for z in range(4)][1:]
    trips.sort(key=lambda t: -sum(min(n, 4 - n) for n in t))

    def goal(trip):
        x, y, z = (lax.rem(v + n, 4) for v, n in zip((side_x, side_y, layer), trip))
        return (x * 4 + y) * 4 + z, {"pat": x * 4 + y, "tile": z * 2 + core}

    def cell(c):
        return (pl.ds(pl.multiple_of(core * 256 + (c // 2) * 8, 8), 8),
                pl.ds(pl.multiple_of(lax.rem(c, 2) * HALF, HALF), HALF))

    own = cell(goal((0, 0, 0))[0])
    swap = remote(pgrad.at[half_of(1 - core), :], half, sum_send, sum_recv, 0, other)
    swap.start()
    low_corner.start()

    @pl.when(core == 0)
    def _():
        out[2].start()
        out[3].start()

    pl.semaphore_wait(inside, pats - 1)
    swap.wait()
    pgrad[half_of(core), :] += half[...]
    for n, trip in enumerate(trips):
        c, device = goal(trip)
        remote(pgrad.at[cell(c)], part.at[n], sum_send, sum_recv, 1, device).start()
    low_corner.wait_send()
    low.start()
    pl.when(core == 1)(out[2].start)
    remote(part, part, sum_send, sum_recv, 1, other).wait()
    acc = pgrad[own]
    for n in range(len(trips)):
        acc = acc + part[n]
    total[own] = acc
    for trip in trips:
        remote(total.at[own], total.at[own], sum_send, sum_recv, 2, goal(trip)[1]).start()

    pl.when(core == 1)(out[3].start)

    @pl.when(core == 0)
    def _():
        low_corner.wait_recv()
        add_corner()

    stores = []

    def finish(k):
        out[k].wait()
        if k == 0:
            low_first.wait()
            low.wait()
            grad[:, :, 0:HALF, 0:256] += from_up[:, :, :, 0:256]
        grad[:, :, chunk[k], 0:HALF] += from_left[:, :, chunk[k], :]
        store = pltpu.make_async_copy(
            grad.at[:, :, chunk[k], pl.ds(0, 256)], out_obj.at[:, :, chunk[k], :], local_sem.at[4 + k])
        store.start()
        stores.append(store)

    finish(1)
    remote(part, part, sum_send, sum_recv, 2, other).wait()
    mine = total.at[half_of(core), :]
    back = remote(mine, mine, sum_send, sum_recv, 3, other)
    back.start()
    finish(2)
    finish(3)
    finish(0)
    back.wait()
    last = pltpu.make_async_copy(total, out_probe, local_sem.at[8])
    last.start()
    for copy in stores:
        copy.wait()
    last.wait()


def on_device(scanned, measured, obj, probe):
    tiles, pats = lax.axis_size("tile"), lax.axis_size("pat")
    table = jnp.asarray(tables())
    anywhere = pl.BlockSpec(memory_space=pl.ANY)
    f32 = jnp.float32
    vmem = lambda *shape: pltpu.VMEM(shape, f32)
    dma = lambda n: pltpu.SemaphoreType.DMA((n,))
    grad_obj, grad_probe = pl.pallas_call(
        functools.partial(kernel, tiles, pats),
        out_shape=[jax.ShapeDtypeStruct(obj.shape, f32), jax.ShapeDtypeStruct((2 * SIDE, SIDE), f32)],
        in_specs=[anywhere] * 5,
        out_specs=[anywhere, anywhere],
        scratch_shapes=[
            pltpu.VMEM(scanned.shape, jnp.int32), vmem(2, 2, 640, 384), vmem(2, 2, 640, 384), vmem(4, 2, SIDE, SIDE), vmem(2, SIDE, SIDE),
            pltpu.VMEM(table.shape, jnp.bfloat16), vmem(2, 2, SIDE, HALF), vmem(2 * SIDE, SIDE),
            vmem(2, 2, 512, HALF), vmem(2, 2, HALF, 384),
            vmem(SIDE, SIDE), vmem(63, 8, HALF), vmem(2 * SIDE, SIDE),
            dma(10), dma(10), dma(10), dma(7), dma(7), dma(4), dma(4), pltpu.SemaphoreType.REGULAR,
        ],
        compiler_params=pltpu.CompilerParams(
            collective_id=0, has_side_effects=True, vmem_limit_bytes=56 * 2**20),
        cost_estimate=pl.CostEstimate(flops=27 * 10**9, bytes_accessed=10 * 2**20, transcendentals=0),
    )(scanned, obj, measured, probe, table)
    return grad_obj, grad_probe.reshape(probe.shape)


def solution(mesh):
    in_specs = (P("tile", "pat"), P("tile", "pat", None, None), P(None, None, "tile", "pat"), P())
    out_specs = (P(None, None, "tile", "pat"), P())
    return jax.shard_map(
        on_device, mesh=mesh, in_specs=in_specs, out_specs=out_specs, check_vma=False
    )
```

```python
import functools

import jax
import jax.numpy as jnp
import ml_dtypes
import numpy as np
from jax import lax
from jax.experimental import pallas as pl
from jax.experimental.pallas import tpu as pltpu
from jax.sharding import PartitionSpec as P

SIDE, HALF = 256, 128
PHASE_SCALE = 40.0

def embed(m):
    return np.block([[m.real, m.imag], [-m.imag, m.real]])

def tables():
    n = np.arange(SIDE)
    dft = np.exp(-2j * np.pi * (n[:, None] * n[None, :] % SIDE) / SIDE) / 16.0
    signed = np.where(n < HALF, n, n - SIDE) / SIDE
    spread = np.exp(-1j * PHASE_SCALE * signed**2)
    move = np.conj(dft) @ (spread[:, None] * dft)
    near, across = move[:HALF, :HALF], move[:HALF, HALF:]
    ce, co = (near + across) / 2, (near - across) / 2
    a, b = dft[:HALF, 0::2], dft[:HALF, 1::2]
    right = [embed(ce), embed(co), embed(a), embed(b), embed(b.T)]
    full = np.stack(right + [m.T for m in right])
    hi = full.astype(ml_dtypes.bfloat16)
    lo = (full - hi.astype(np.float64)).astype(ml_dtypes.bfloat16)
    order = np.concatenate([np.arange(0, SIDE, 2), np.arange(1, SIDE, 2)])
    perm = np.zeros((SIDE, SIDE))
    perm[order, n] = 1.0
    return np.concatenate([hi, lo, perm[None].astype(ml_dtypes.bfloat16)])

CE, CO, FA, FB, FBT = range(5)
LEFT = 5
LOW = 10
PERM = 20

def split(x):
    hi = x.astype(jnp.bfloat16)
    return hi, (x - hi.astype(jnp.float32)).astype(jnp.bfloat16)

def dot(l, r):
    return jnp.dot(l, r, preferred_element_type=jnp.float32)

def mul_right(x, tab, k):
    hi, lo = split(x)
    wh, wl = tab[k], tab[k + LOW]
    return dot(hi, wh) + dot(lo, wh) + dot(hi, wl)

def mul_left(x, tab, k):
    hi, lo = split(x)
    wh, wl = tab[k + LEFT], tab[k + LEFT + LOW]
    return dot(wh, hi) + dot(wl, hi) + dot(wh, lo)

def lanes(re, im):
    rl, rr, il, ir = re[:, :HALF], re[:, HALF:], im[:, :HALF], im[:, HALF:]
    cat = lambda p, q: jnp.concatenate([p, q], axis=1)
    return cat(rl + rr, il + ir), cat(rl - rr, il - ir)

def rows(re, im):
    rt, rb, it, ib = re[:HALF], re[HALF:], im[:HALF], im[HALF:]
    cat = lambda p, q: jnp.concatenate([p, q], axis=0)
    return cat(rt + rb, it + ib), cat(rt - rb, it - ib)

def planes_of_lanes(even, odd):
    re = jnp.concatenate([even[:, :HALF], odd[:, :HALF]], axis=1)
    im = jnp.concatenate([even[:, HALF:], odd[:, HALF:]], axis=1)
    return re, im

def planes_of_rows(even, odd):
    re = jnp.concatenate([even[:HALF], odd[:HALF]], axis=0)
    im = jnp.concatenate([even[HALF:], odd[HALF:]], axis=0)
    return re, im

def spread(re, im, tab):
    e, o = lanes(re, im)
    e, o = mul_right(e, tab, CE), mul_right(o, tab, CO)
    yield
    re, im = planes_of_lanes(e, o)
    e, o = rows(re, im)
    e, o = mul_left(e, tab, CE), mul_left(o, tab, CO)
    yield
    re, im = planes_of_rows(e + o, e - o)
    l = lambda t: jnp.concatenate([t[:, :HALF] + t[:, HALF:], t[:, :HALF] - t[:, HALF:]], axis=1)
    return l(re), l(im)

def to_far(re, im, tab):
    e, o = lanes(re, im)
    e, o = mul_right(e, tab, FA), mul_right(o, tab, FB)
    yield
    re, im = planes_of_lanes(e, o)
    e, o = rows(re, im)
    e, o = mul_left(e, tab, FA), mul_left(o, tab, FB)
    yield
    return e, o

def from_far(even, odd, tab):
    e, o = mul_left(even, tab, FA), mul_left(odd, tab, FBT)
    yield
    re, im = planes_of_rows(e + o, e - o)
    e = jnp.concatenate([re[:, :HALF], im[:, :HALF]], axis=1)
    o = jnp.concatenate([re[:, HALF:], im[:, HALF:]], axis=1)
    e, o = mul_right(e, tab, FA), mul_right(o, tab, FBT)
    yield
    return planes_of_lanes(e + o, e - o)

def point(scanned, pad, grad, meas, probe, pgrad, tab, order, a, b):
    r = pl.ds(pl.multiple_of(a * HALF, HALF), SIDE)
    c = pl.ds(pl.multiple_of(b * HALF, HALF), SIDE)
    here = [lax.broadcasted_iota(jnp.int32, scanned.shape, n) == v for n, v in enumerate((b, a))]
    live = jnp.where(here[0] & here[1], scanned[...].astype(jnp.float32), 0.0)
    weight = jnp.sum(jnp.sum(live, axis=1, keepdims=True), axis=0, keepdims=True)
    pr, pi = probe[0], probe[1]
    o0r, o0i = pad[0, 0, r, c], pad[0, 1, r, c]
    ur, ui = yield from spread(pr * o0r - pi * o0i, pr * o0i + pi * o0r, tab)
    o1r, o1i = pad[1, 0, r, c], pad[1, 1, r, c]
    even, odd = yield from to_far(ur * o1r - ui * o1i, ur * o1i + ui * o1r, tab)
    hi, lo = split(meas[a, b])
    m = dot(hi, tab[PERM]) + dot(lo, tab[PERM])
    order[0], order[1] = m[:, :HALF], m[:, HALF:]

    def pull(f, start):
        pick = pl.ds(start, HALF, stride=2)
        m = jnp.concatenate([order[0, pick, :], order[1, pick, :]], axis=1)
        fr, fi = f[:HALF], f[HALF:]
        d = (fr * fr + fi * fi - m) * (2.0 * weight)
        return jnp.concatenate([d * fr, -(d * fi)], axis=0)

    gr, gi = yield from from_far(pull(even, 0), pull(odd, 1), tab)
    grad[1, 0, r, c] += ur * gr - ui * gi
    grad[1, 1, r, c] -= ur * gi + ui * gr
    o1r, o1i = pad[1, 0, r, c], pad[1, 1, r, c]
    gr, gi = yield from spread(o1r * gr - o1i * gi, o1r * gi + o1i * gr, tab)
    pr, pi = probe[0], probe[1]
    grad[0, 0, r, c] += pr * gr - pi * gi
    grad[0, 1, r, c] -= pr * gi + pi * gr
    o0r, o0i = pad[0, 0, r, c], pad[0, 1, r, c]
    pgrad[0:SIDE] += o0r * gr - o0i * gi
    pgrad[SIDE:] -= o0r * gi + o0i * gr


def run(work):
    work = list(work)
    while work:
        for w in list(work):
            if next(w, work) is work:
                work.remove(w)


MESH = pl.DeviceIdType.MESH


def kernel(tiles, pats, scanned_in, obj, meas_in, probe_in, tab_in, out_obj, out_probe,
           scanned, pad, grad, meas, probe, tab, order, pgrad, from_left, from_up, half, part, total,
           local_sem, halo_send, halo_recv, grad_send, grad_recv, sum_send, sum_recv, inside):
    tile, pat = lax.axis_index("tile"), lax.axis_index("pat")
    left, right = {"pat": lax.rem(pat + pats - 1, pats)}, {"pat": lax.rem(pat + 1, pats)}
    up, down = {"tile": lax.rem(tile + tiles - 1, tiles)}, {"tile": lax.rem(tile + 1, tiles)}

    def remote(src, dst, send, recv, k, device):
        return pltpu.make_async_remote_copy(
            src_ref=src, dst_ref=dst, send_sem=send.at[k], recv_sem=recv.at[k],
            device_id=device, device_id_type=MESH)

    loads = [
        pltpu.make_async_copy(obj, pad.at[:, :, pl.ds(0, 512), pl.ds(0, 256)], local_sem.at[0]),
        pltpu.make_async_copy(probe_in, probe, local_sem.at[1]),
        pltpu.make_async_copy(tab_in, tab, local_sem.at[2]),
        pltpu.make_async_copy(meas_in, meas, local_sem.at[3]),
        pltpu.make_async_copy(scanned_in, scanned, local_sem.at[9]),
    ]
    for copy in loads:
        copy.start()

    barrier = pltpu.get_barrier_semaphore()
    for o in range(1, tiles):
        pl.semaphore_signal(barrier, inc=1, device_id={"tile": lax.rem(tile + o, tiles)}, device_id_type=MESH)
    for o in range(1, pats):
        pl.semaphore_signal(barrier, inc=1, device_id={"pat": lax.rem(pat + o, pats)}, device_id_type=MESH)
    grad[...] = jnp.zeros_like(grad)
    pgrad[...] = jnp.zeros_like(pgrad)
    pl.semaphore_wait(barrier, tiles - 1 + pats - 1)

    first, second = pl.ds(0, HALF), pl.ds(256, HALF)
    chunk = [pl.ds(k * HALF, HALF) for k in range(5)]
    piece = [pl.ds(k * 64, 64) for k in range(8)]
    beside = [
        remote(obj.at[:, :, piece[k], first], pad.at[:, :, piece[k], second], halo_send, halo_recv, k, left)
        for k in range(8)
    ]
    below = remote(obj.at[:, :, chunk[0], :], pad.at[:, :, chunk[4], pl.ds(0, 256)], halo_send, halo_recv, 8, up)
    corner = remote(pad.at[:, :, chunk[0], second], pad.at[:, :, chunk[4], second], halo_send, halo_recv, 9, up)
    core = lax.rem(tile, 2)

    @pl.when(core == 0)
    def _():
        for k in range(8):
            beside[k].start()

    below.start()
    for copy in loads:
        copy.wait()

    low_first = remote(
        grad.at[:, :, chunk[4], first], from_up.at[:, :, :, first], grad_send, grad_recv, 6, down)
    low = remote(
        grad.at[:, :, chunk[4], chunk[1]], from_up.at[:, :, :, chunk[1]], grad_send, grad_recv, 4, down)
    low_corner = remote(
        grad.at[:, :, chunk[4], second], from_up.at[:, :, :, second], grad_send, grad_recv, 5, down)
    out = [
        remote(grad.at[:, :, chunk[k], second], from_left.at[:, :, chunk[k], :], grad_send, grad_recv, k, right)
        for k in range(4)
    ]

    def add_corner():
        grad[:, :, 0:HALF, 256:] += from_up[:, :, :, 256:]
        out[0].start()

    def step(i, _):
        @pl.when(i == 1)
        def _():
            below.wait()

        @pl.when(i == 2)
        def _():
            @pl.when(core == 1)
            def _():
                for k in range(3):
                    beside[k].start()

            for o in range(1, pats):
                pl.semaphore_signal(inside, inc=1, device_id={"pat": lax.rem(pat + o, pats)}, device_id_type=MESH)
            low_first.start()
            for k in range(5):
                beside[k].wait_send()
                pl.when(core == 1)(beside[k + 3].start)
                if k == 2:
                    beside[0].wait_recv()
                    beside[1].wait_recv()
                    corner.start()
            for k in range(2, 6):
                beside[k].wait_recv()

        @pl.when(i == 3)
        def _():
            out[1].start()

            @pl.when(core == 1)
            def _():
                low_corner.wait_recv()
                add_corner()

            for k in range(5, 8):
                beside[k].wait_send()
            beside[6].wait_recv()
            beside[7].wait_recv()
            corner.wait()

        b = i // 2
        a = 2 * i - 4 * b
        run(
            point(scanned, pad, grad, meas, probe, pgrad, tab, order.at[k], a + k, b)
            for k in range(2)
        )
        return 0

    lax.fori_loop(0, 4, step, 0)

    other = {"tile": tile + 1 - 2 * core}
    layer, side_x, side_y = tile // 2, pat // 4, lax.rem(pat, 4)
    half_of = lambda c: pl.ds(pl.multiple_of(c * 256, 256), 256)
    trips = [(x, y, z) for x in range(4) for y in range(4) for z in range(4)][1:]
    trips.sort(key=lambda t: -sum(min(n, 4 - n) for n in t))

    def goal(trip):
        x, y, z = (lax.rem(v + n, 4) for v, n in zip((side_x, side_y, layer), trip))
        return (x * 4 + y) * 4 + z, {"pat": x * 4 + y, "tile": z * 2 + core}

    def cell(c):
        return (pl.ds(pl.multiple_of(core * 256 + (c // 2) * 8, 8), 8),
                pl.ds(pl.multiple_of(lax.rem(c, 2) * HALF, HALF), HALF))

    own = cell(goal((0, 0, 0))[0])
    swap = remote(pgrad.at[half_of(1 - core), :], half, sum_send, sum_recv, 0, other)
    swap.start()
    low_corner.start()

    @pl.when(core == 0)
    def _():
        out[2].start()
        out[3].start()

    pl.semaphore_wait(inside, pats - 1)
    swap.wait()
    pgrad[half_of(core), :] += half[...]
    for n, trip in enumerate(trips):
        c, device = goal(trip)
        remote(pgrad.at[cell(c)], part.at[n], sum_send, sum_recv, 1, device).start()
    low_corner.wait_send()
    low.start()
    pl.when(core == 1)(out[2].start)
    remote(part, part, sum_send, sum_recv, 1, other).wait()
    acc = pgrad[own]
    for n in range(len(trips)):
        acc = acc + part[n]
    total[own] = acc
    for trip in trips:
        remote(total.at[own], total.at[own], sum_send, sum_recv, 2, goal(trip)[1]).start()

    pl.when(core == 1)(out[3].start)

    @pl.when(core == 0)
    def _():
        low_corner.wait_recv()
        add_corner()

    def finish(k):
        out[k].wait()
        if k == 0:
            low_first.wait()
            low.wait()
            grad[:, :, 0:HALF, 0:256] += from_up[:, :, :, 0:256]
        out_obj[:, :, chunk[k], 0:HALF] = grad[:, :, chunk[k], 0:HALF] + from_left[:, :, chunk[k], :]
        out_obj[:, :, chunk[k], HALF:] = grad[:, :, chunk[k], HALF:256]

    finish(1)
    remote(part, part, sum_send, sum_recv, 2, other).wait()
    mine = half_of(core)
    back = remote(total.at[mine, :], out_probe.at[core], sum_send, sum_recv, 3, other)
    back.start()
    out_probe[core] = total[mine, :]
    finish(2)
    finish(3)
    finish(0)
    back.wait()


def on_device(scanned, measured, obj, probe):
    tiles, pats = lax.axis_size("tile"), lax.axis_size("pat")
    table = jnp.asarray(tables())
    anywhere = pl.BlockSpec(memory_space=pl.ANY)
    f32 = jnp.float32
    vmem = lambda *shape: pltpu.VMEM(shape, f32)
    dma = lambda n: pltpu.SemaphoreType.DMA((n,))
    grad_obj, grad_probe = pl.pallas_call(
        functools.partial(kernel, tiles, pats),
        out_shape=[pltpu.VMEM(obj.shape, f32), pltpu.VMEM(probe.shape, f32)],
        in_specs=[anywhere] * 5,
        out_specs=[pl.BlockSpec(memory_space=pltpu.VMEM)] * 2,
        scratch_shapes=[
            pltpu.VMEM(scanned.T.shape, jnp.int32), vmem(2, 2, 640, 384), vmem(2, 2, 640, 384), vmem(4, 2, SIDE, SIDE), vmem(2, SIDE, SIDE),
            pltpu.VMEM(table.shape, jnp.bfloat16), vmem(2, 2, SIDE, HALF), vmem(2 * SIDE, SIDE),
            vmem(2, 2, 512, HALF), vmem(2, 2, HALF, 384),
            vmem(SIDE, SIDE), vmem(63, 8, HALF), vmem(2 * SIDE, SIDE),
            dma(10), dma(10), dma(10), dma(7), dma(7), dma(4), dma(4), pltpu.SemaphoreType.REGULAR,
        ],
        compiler_params=pltpu.CompilerParams(
            collective_id=0, has_side_effects=True, vmem_limit_bytes=56 * 2**20),
        cost_estimate=pl.CostEstimate(flops=27 * 10**9, bytes_accessed=10 * 2**20, transcendentals=0),
    )(scanned.T, obj, measured, probe, table)
    return grad_obj, grad_probe


def solution(mesh):
    in_specs = (P("tile", "pat"), P("tile", "pat", None, None), P(None, None, "tile", "pat"), P())
    out_specs = (P(None, None, "tile", "pat"), P())
    return jax.shard_map(
        on_device, mesh=mesh, in_specs=in_specs, out_specs=out_specs, check_vma=False
    )
```

```python
import functools

import jax
import jax.numpy as jnp
import ml_dtypes
import numpy as np
from jax import lax
from jax.experimental import pallas as pl
from jax.experimental.pallas import tpu as pltpu
from jax.sharding import PartitionSpec as P

SIDE, HALF = 256, 128
PHASE_SCALE = 40.0

def embed(m):
    return np.block([[m.real, m.imag], [-m.imag, m.real]])

def tables():
    n = np.arange(SIDE)
    dft = np.exp(-2j * np.pi * (n[:, None] * n[None, :] % SIDE) / SIDE) / 16.0
    signed = np.where(n < HALF, n, n - SIDE) / SIDE
    spread = np.exp(-1j * PHASE_SCALE * signed**2)
    move = np.conj(dft) @ (spread[:, None] * dft)
    near, across = move[:HALF, :HALF], move[:HALF, HALF:]
    ce, co = (near + across) / 2, (near - across) / 2
    a, b = dft[:HALF, 0::2], dft[:HALF, 1::2]
    right = [embed(ce), embed(co), embed(a), embed(b), embed(b.T)]
    full = np.stack(right + [m.T for m in right])
    hi = full.astype(ml_dtypes.bfloat16)
    lo = (full - hi.astype(np.float64)).astype(ml_dtypes.bfloat16)
    order = np.concatenate([np.arange(0, SIDE, 2), np.arange(1, SIDE, 2)])
    perm = np.zeros((SIDE, SIDE))
    perm[order, n] = 1.0
    return np.concatenate([hi, lo, perm[None].astype(ml_dtypes.bfloat16)])

CE, CO, FA, FB, FBT = range(5)
LEFT = 5
LOW = 10
PERM = 20

def split(x):
    hi = x.astype(jnp.bfloat16)
    return hi, (x - hi.astype(jnp.float32)).astype(jnp.bfloat16)

def dot(l, r):
    return jnp.dot(l, r, preferred_element_type=jnp.float32)

def mul_right(x, tab, k):
    hi, lo = split(x)
    wh, wl = tab[k], tab[k + LOW]
    return dot(hi, wh) + dot(lo, wh) + dot(hi, wl)

def mul_left(x, tab, k):
    hi, lo = split(x)
    wh, wl = tab[k + LEFT], tab[k + LEFT + LOW]
    both = dot(jnp.concatenate([wh, wl], axis=0), hi)
    return both[:SIDE] + both[SIDE:] + dot(wh, lo)

def lanes(re, im):
    rl, rr, il, ir = re[:, :HALF], re[:, HALF:], im[:, :HALF], im[:, HALF:]
    cat = lambda p, q: jnp.concatenate([p, q], axis=1)
    return cat(rl + rr, il + ir), cat(rl - rr, il - ir)

def rows(re, im):
    rt, rb, it, ib = re[:HALF], re[HALF:], im[:HALF], im[HALF:]
    cat = lambda p, q: jnp.concatenate([p, q], axis=0)
    return cat(rt + rb, it + ib), cat(rt - rb, it - ib)

def planes_of_lanes(even, odd):
    re = jnp.concatenate([even[:, :HALF], odd[:, :HALF]], axis=1)
    im = jnp.concatenate([even[:, HALF:], odd[:, HALF:]], axis=1)
    return re, im

def planes_of_rows(even, odd):
    re = jnp.concatenate([even[:HALF], odd[:HALF]], axis=0)
    im = jnp.concatenate([even[HALF:], odd[HALF:]], axis=0)
    return re, im

def spread(re, im, tab):
    e, o = lanes(re, im)
    e, o = mul_right(e, tab, CE), mul_right(o, tab, CO)
    yield
    re, im = planes_of_lanes(e, o)
    e, o = rows(re, im)
    e, o = mul_left(e, tab, CE), mul_left(o, tab, CO)
    yield
    re, im = planes_of_rows(e + o, e - o)
    l = lambda t: jnp.concatenate([t[:, :HALF] + t[:, HALF:], t[:, :HALF] - t[:, HALF:]], axis=1)
    return l(re), l(im)

def to_far(re, im, tab):
    e, o = lanes(re, im)
    e, o = mul_right(e, tab, FA), mul_right(o, tab, FB)
    yield
    re, im = planes_of_lanes(e, o)
    e, o = rows(re, im)
    e, o = mul_left(e, tab, FA), mul_left(o, tab, FB)
    yield
    return e, o

def from_far(even, odd, tab):
    e, o = mul_left(even, tab, FA), mul_left(odd, tab, FBT)
    yield
    re, im = planes_of_rows(e + o, e - o)
    e = jnp.concatenate([re[:, :HALF], im[:, :HALF]], axis=1)
    o = jnp.concatenate([re[:, HALF:], im[:, HALF:]], axis=1)
    e, o = mul_right(e, tab, FA), mul_right(o, tab, FBT)
    yield
    return planes_of_lanes(e + o, e - o)

def point(scanned, pad, grad, meas, probe, pgrad, tab, order, a, b):
    r = pl.ds(pl.multiple_of(a * HALF, HALF), SIDE)
    c = pl.ds(pl.multiple_of(b * HALF, HALF), SIDE)
    here = [lax.broadcasted_iota(jnp.int32, scanned.shape, n) == v for n, v in enumerate((b, a))]
    live = jnp.where(here[0] & here[1], scanned[...].astype(jnp.float32), 0.0)
    weight = jnp.sum(jnp.sum(live, axis=1, keepdims=True), axis=0, keepdims=True)
    pr, pi = probe[0], probe[1]
    o0r, o0i = pad[0, 0, r, c], pad[0, 1, r, c]
    ur, ui = yield from spread(pr * o0r - pi * o0i, pr * o0i + pi * o0r, tab)
    o1r, o1i = pad[1, 0, r, c], pad[1, 1, r, c]
    even, odd = yield from to_far(ur * o1r - ui * o1i, ur * o1i + ui * o1r, tab)
    hi, lo = split(meas[a, b])
    m = dot(hi, tab[PERM]) + dot(lo, tab[PERM])
    order[0], order[1] = m[:, :HALF], m[:, HALF:]

    def pull(f, start):
        pick = pl.ds(start, HALF, stride=2)
        m = jnp.concatenate([order[0, pick, :], order[1, pick, :]], axis=1)
        fr, fi = f[:HALF], f[HALF:]
        d = (fr * fr + fi * fi - m) * (2.0 * weight)
        return jnp.concatenate([d * fr, -(d * fi)], axis=0)

    gr, gi = yield from from_far(pull(even, 0), pull(odd, 1), tab)
    grad[1, 0, r, c] += ur * gr - ui * gi
    grad[1, 1, r, c] -= ur * gi + ui * gr
    o1r, o1i = pad[1, 0, r, c], pad[1, 1, r, c]
    gr, gi = yield from spread(o1r * gr - o1i * gi, o1r * gi + o1i * gr, tab)
    pr, pi = probe[0], probe[1]
    grad[0, 0, r, c] += pr * gr - pi * gi
    grad[0, 1, r, c] -= pr * gi + pi * gr
    o0r, o0i = pad[0, 0, r, c], pad[0, 1, r, c]
    pgrad[0:SIDE] += o0r * gr - o0i * gi
    pgrad[SIDE:] -= o0r * gi + o0i * gr


def run(work):
    work = list(work)
    while work:
        for w in list(work):
            if next(w, work) is work:
                work.remove(w)


MESH = pl.DeviceIdType.MESH


def kernel(tiles, pats, scanned_in, obj, meas_in, probe_in, tab_in, out_obj, out_probe,
           scanned, pad, grad, meas, probe, tab, order, pgrad, from_left, from_up, half, part, total,
           local_sem, halo_send, halo_recv, grad_send, grad_recv, sum_send, sum_recv, inside):
    tile, pat = lax.axis_index("tile"), lax.axis_index("pat")
    left, right = {"pat": lax.rem(pat + pats - 1, pats)}, {"pat": lax.rem(pat + 1, pats)}
    up, down = {"tile": lax.rem(tile + tiles - 1, tiles)}, {"tile": lax.rem(tile + 1, tiles)}

    def remote(src, dst, send, recv, k, device):
        return pltpu.make_async_remote_copy(
            src_ref=src, dst_ref=dst, send_sem=send.at[k], recv_sem=recv.at[k],
            device_id=device, device_id_type=MESH)

    loads = [
        pltpu.make_async_copy(obj, pad.at[:, :, pl.ds(0, 512), pl.ds(0, 256)], local_sem.at[0]),
        pltpu.make_async_copy(probe_in, probe, local_sem.at[1]),
        pltpu.make_async_copy(tab_in, tab, local_sem.at[2]),
        pltpu.make_async_copy(meas_in, meas, local_sem.at[3]),
        pltpu.make_async_copy(scanned_in, scanned, local_sem.at[9]),
    ]
    barrier = pltpu.get_barrier_semaphore()
    side_x, side_y = pat // 4, lax.rem(pat, 4)
    along_x = [{"pat": lax.rem(side_x + n, 4) * 4 + side_y} for n in (1, 2, 3)]
    along_y = [{"pat": side_x * 4 + lax.rem(side_y + n, 4)} for n in (1, 2, 3)]
    along_tile = [{"tile": lax.rem(tile + o, tiles)} for o in (1, tiles - 1, 2, 3, 4, 5, 6)]
    for device in [left, right] + along_y + along_x + along_tile:
        pl.semaphore_signal(barrier, inc=1, device_id=device, device_id_type=MESH)
    pl.semaphore_wait(barrier, tiles - 1 + 8)

    first, second = pl.ds(0, HALF), pl.ds(256, HALF)
    chunk = [pl.ds(k * HALF, HALF) for k in range(5)]
    piece = [pl.ds(k * 64, 64) for k in range(8)]
    beside = [
        remote(obj.at[:, :, piece[k], first], pad.at[:, :, piece[k], second], halo_send, halo_recv, k, left)
        for k in range(8)
    ]
    below = remote(obj.at[:, :, chunk[0], :], pad.at[:, :, chunk[4], pl.ds(0, 256)], halo_send, halo_recv, 8, up)
    corner = remote(pad.at[:, :, chunk[0], second], pad.at[:, :, chunk[4], second], halo_send, halo_recv, 9, up)
    core = lax.rem(tile, 2)

    @pl.when(core == 0)
    def _():
        for k in range(8):
            beside[k].start()

    below.start()
    for copy in loads:
        copy.start()
    grad[...] = jnp.zeros_like(grad)
    pgrad[...] = jnp.zeros_like(pgrad)
    for copy in loads:
        copy.wait()

    low_first = remote(
        grad.at[:, :, chunk[4], first], from_up.at[:, :, :, first], grad_send, grad_recv, 6, down)
    low = remote(
        grad.at[:, :, chunk[4], chunk[1]], from_up.at[:, :, :, chunk[1]], grad_send, grad_recv, 4, down)
    low_corner = remote(
        grad.at[:, :, chunk[4], second], from_up.at[:, :, :, second], grad_send, grad_recv, 5, down)
    out = [
        remote(grad.at[:, :, chunk[k], second], from_left.at[:, :, chunk[k], :], grad_send, grad_recv, k, right)
        for k in range(4)
    ]

    def add_corner():
        grad[:, :, 0:HALF, 256:] += from_up[:, :, :, 256:]
        out[0].start()

    def step(i, _):
        @pl.when(i == 1)
        def _():
            below.wait()

        @pl.when(i == 2)
        def _():
            @pl.when(core == 1)
            def _():
                for k in range(3):
                    beside[k].start()

            for device in along_y:
                pl.semaphore_signal(inside.at[0], inc=1, device_id=device, device_id_type=MESH)
            low_first.start()
            for k in range(5):
                beside[k].wait_send()
                pl.when(core == 1)(beside[k + 3].start)
                if k == 2:
                    beside[0].wait_recv()
                    beside[1].wait_recv()
                    corner.start()
            for k in range(2, 6):
                beside[k].wait_recv()

        @pl.when(i == 3)
        def _():
            out[1].start()
            pl.semaphore_wait(inside.at[0], 3)
            for device in along_x:
                pl.semaphore_signal(inside.at[1], inc=1, device_id=device, device_id_type=MESH)

            @pl.when(core == 1)
            def _():
                low_corner.wait_recv()
                add_corner()

            for k in range(5, 8):
                beside[k].wait_send()
            beside[6].wait_recv()
            beside[7].wait_recv()
            corner.wait()

        b = i // 2
        a = 2 * i - 4 * b
        run(
            point(scanned, pad, grad, meas, probe, pgrad, tab, order.at[k], a + k, b)
            for k in range(2)
        )
        return 0

    lax.fori_loop(0, 4, step, 0)

    other = {"tile": tile + 1 - 2 * core}
    layer = tile // 2
    half_of = lambda c: pl.ds(pl.multiple_of(c * 256, 256), 256)
    trips = [(x, y, z) for x in range(4) for y in range(4) for z in range(4)][1:]
    trips.sort(key=lambda t: -sum(min(n, 4 - n) for n in t))

    def goal(trip):
        x, y, z = (lax.rem(v + n, 4) for v, n in zip((side_x, side_y, layer), trip))
        return (x * 4 + y) * 4 + z, {"pat": x * 4 + y, "tile": z * 2 + core}

    def cell(c):
        return (pl.ds(pl.multiple_of(core * 256 + (c // 2) * 8, 8), 8),
                pl.ds(pl.multiple_of(lax.rem(c, 2) * HALF, HALF), HALF))

    own = cell(goal((0, 0, 0))[0])
    swap = remote(pgrad.at[half_of(1 - core), :], half, sum_send, sum_recv, 0, other)
    swap.start()
    low_corner.start()

    @pl.when(core == 0)
    def _():
        out[2].start()
        out[3].start()

    pl.semaphore_wait(inside.at[1], 3)
    swap.wait()
    pgrad[half_of(core), :] += half[...]
    for n, trip in enumerate(trips):
        c, device = goal(trip)
        remote(pgrad.at[cell(c)], part.at[n], sum_send, sum_recv, 1, device).start()
    low_corner.wait_send()
    low.start()
    pl.when(core == 1)(out[2].start)
    remote(part, part, sum_send, sum_recv, 1, other).wait()
    acc = pgrad[own]
    for n in range(len(trips)):
        acc = acc + part[n]
    total[own] = acc
    for trip in trips:
        remote(total.at[own], total.at[own], sum_send, sum_recv, 2, goal(trip)[1]).start()

    pl.when(core == 1)(out[3].start)

    @pl.when(core == 0)
    def _():
        low_corner.wait_recv()
        add_corner()

    def finish(k):
        out[k].wait()
        if k == 0:
            low_first.wait()
            low.wait()
            grad[:, :, 0:HALF, 0:256] += from_up[:, :, :, 0:256]
        out_obj[:, :, chunk[k], 0:HALF] = grad[:, :, chunk[k], 0:HALF] + from_left[:, :, chunk[k], :]
        out_obj[:, :, chunk[k], HALF:] = grad[:, :, chunk[k], HALF:256]

    finish(1)
    remote(part, part, sum_send, sum_recv, 2, other).wait()
    mine = half_of(core)
    back = remote(total.at[mine, :], out_probe.at[core], sum_send, sum_recv, 3, other)
    back.start()
    out_probe[core] = total[mine, :]
    finish(2)
    finish(3)
    finish(0)
    back.wait()


def on_device(scanned, measured, obj, probe):
    tiles, pats = lax.axis_size("tile"), lax.axis_size("pat")
    table = jnp.asarray(tables())
    anywhere = pl.BlockSpec(memory_space=pl.ANY)
    f32 = jnp.float32
    vmem = lambda *shape: pltpu.VMEM(shape, f32)
    dma = lambda n: pltpu.SemaphoreType.DMA((n,))
    grad_obj, grad_probe = pl.pallas_call(
        functools.partial(kernel, tiles, pats),
        out_shape=[pltpu.VMEM(obj.shape, f32), pltpu.VMEM(probe.shape, f32)],
        in_specs=[anywhere] * 5,
        out_specs=[pl.BlockSpec(memory_space=pltpu.VMEM)] * 2,
        scratch_shapes=[
            pltpu.VMEM(scanned.T.shape, jnp.int32), vmem(2, 2, 640, 384), vmem(2, 2, 640, 384), vmem(4, 2, SIDE, SIDE), vmem(2, SIDE, SIDE),
            pltpu.VMEM(table.shape, jnp.bfloat16), vmem(2, 2, SIDE, HALF), vmem(2 * SIDE, SIDE),
            vmem(2, 2, 512, HALF), vmem(2, 2, HALF, 384),
            vmem(SIDE, SIDE), vmem(63, 8, HALF), vmem(2 * SIDE, SIDE),
            dma(10), dma(10), dma(10), dma(7), dma(7), dma(4), dma(4), pltpu.SemaphoreType.REGULAR((2,)),
        ],
        compiler_params=pltpu.CompilerParams(
            collective_id=0, has_side_effects=True, vmem_limit_bytes=56 * 2**20),
        cost_estimate=pl.CostEstimate(flops=27 * 10**9, bytes_accessed=10 * 2**20, transcendentals=0),
    )(scanned.T, obj, measured, probe, table)
    return grad_obj, grad_probe


def solution(mesh):
    in_specs = (P("tile", "pat"), P("tile", "pat", None, None), P(None, None, "tile", "pat"), P())
    out_specs = (P(None, None, "tile", "pat"), P())
    return jax.shard_map(
        on_device, mesh=mesh, in_specs=in_specs, out_specs=out_specs, check_vma=False
    )
```

```python
import functools

import jax
import jax.numpy as jnp
import ml_dtypes
import numpy as np
from jax import lax
from jax.experimental import pallas as pl
from jax.experimental.pallas import tpu as pltpu
from jax.sharding import PartitionSpec as P

SIDE, HALF = 256, 128
PHASE_SCALE = 40.0

def embed(m):
    return np.block([[m.real, m.imag], [-m.imag, m.real]])

def tables():
    n = np.arange(SIDE)
    dft = np.exp(-2j * np.pi * (n[:, None] * n[None, :] % SIDE) / SIDE) / 16.0
    signed = np.where(n < HALF, n, n - SIDE) / SIDE
    spread = np.exp(-1j * PHASE_SCALE * signed**2)
    move = np.conj(dft) @ (spread[:, None] * dft)
    near, across = move[:HALF, :HALF], move[:HALF, HALF:]
    ce, co = (near + across) / 2, (near - across) / 2
    a, b = dft[:HALF, 0::2], dft[:HALF, 1::2]
    right = [embed(ce), embed(co), embed(a), embed(b), embed(b.T)]
    full = np.stack(right + [m.T for m in right])
    hi = full.astype(ml_dtypes.bfloat16)
    lo = (full - hi.astype(np.float64)).astype(ml_dtypes.bfloat16)
    order = np.concatenate([np.arange(0, SIDE, 2), np.arange(1, SIDE, 2)])
    perm = np.zeros((SIDE, SIDE))
    perm[order, n] = 1.0
    return np.concatenate([hi, lo, perm[None].astype(ml_dtypes.bfloat16)])

CE, CO, FA, FB, FBT = range(5)
LEFT = 5
LOW = 10
PERM = 20

def split(x):
    hi = x.astype(jnp.bfloat16)
    return hi, (x - hi.astype(jnp.float32)).astype(jnp.bfloat16)

def dot(l, r):
    return jnp.dot(l, r, preferred_element_type=jnp.float32)

def mul_right(x, tab, k):
    hi, lo = split(x)
    wh, wl = tab[k], tab[k + LOW]
    return dot(hi, wh) + dot(lo, wh) + dot(hi, wl)

def mul_left(x, tab, k):
    hi, lo = split(x)
    wh, wl = tab[k + LEFT], tab[k + LEFT + LOW]
    both = dot(jnp.concatenate([wh, wl], axis=0), hi)
    return both[:SIDE] + both[SIDE:] + dot(wh, lo)

def lanes(re, im):
    rl, rr, il, ir = re[:, :HALF], re[:, HALF:], im[:, :HALF], im[:, HALF:]
    cat = lambda p, q: jnp.concatenate([p, q], axis=1)
    return cat(rl + rr, il + ir), cat(rl - rr, il - ir)

def rows(re, im):
    rt, rb, it, ib = re[:HALF], re[HALF:], im[:HALF], im[HALF:]
    cat = lambda p, q: jnp.concatenate([p, q], axis=0)
    return cat(rt + rb, it + ib), cat(rt - rb, it - ib)

def planes_of_lanes(even, odd):
    re = jnp.concatenate([even[:, :HALF], odd[:, :HALF]], axis=1)
    im = jnp.concatenate([even[:, HALF:], odd[:, HALF:]], axis=1)
    return re, im

def planes_of_rows(even, odd):
    re = jnp.concatenate([even[:HALF], odd[:HALF]], axis=0)
    im = jnp.concatenate([even[HALF:], odd[HALF:]], axis=0)
    return re, im

def spread(re, im, tab):
    e, o = lanes(re, im)
    e, o = mul_right(e, tab, CE), mul_right(o, tab, CO)
    yield
    re, im = planes_of_lanes(e, o)
    e, o = rows(re, im)
    e, o = mul_left(e, tab, CE), mul_left(o, tab, CO)
    yield
    re, im = planes_of_rows(e + o, e - o)
    l = lambda t: jnp.concatenate([t[:, :HALF] + t[:, HALF:], t[:, :HALF] - t[:, HALF:]], axis=1)
    return l(re), l(im)

def to_far(re, im, tab):
    e, o = lanes(re, im)
    e, o = mul_right(e, tab, FA), mul_right(o, tab, FB)
    yield
    re, im = planes_of_lanes(e, o)
    e, o = rows(re, im)
    e, o = mul_left(e, tab, FA), mul_left(o, tab, FB)
    yield
    return e, o

def from_far(even, odd, tab):
    e, o = mul_left(even, tab, FA), mul_left(odd, tab, FBT)
    yield
    re, im = planes_of_rows(e + o, e - o)
    e = jnp.concatenate([re[:, :HALF], im[:, :HALF]], axis=1)
    o = jnp.concatenate([re[:, HALF:], im[:, HALF:]], axis=1)
    e, o = mul_right(e, tab, FA), mul_right(o, tab, FBT)
    yield
    return planes_of_lanes(e + o, e - o)

def point(scanned, pad, grad, meas, probe, pgrad, tab, order, a, b):
    r = pl.ds(pl.multiple_of(a * HALF, HALF), SIDE)
    c = pl.ds(pl.multiple_of(b * HALF, HALF), SIDE)
    here = [lax.broadcasted_iota(jnp.int32, scanned.shape, n) == v for n, v in enumerate((b, a))]
    live = jnp.where(here[0] & here[1], scanned[...].astype(jnp.float32), 0.0)
    weight = jnp.sum(jnp.sum(live, axis=1, keepdims=True), axis=0, keepdims=True)
    pr, pi = probe[0], probe[1]
    o0r, o0i = pad[0, 0, r, c], pad[0, 1, r, c]
    ur, ui = yield from spread(pr * o0r - pi * o0i, pr * o0i + pi * o0r, tab)
    o1r, o1i = pad[1, 0, r, c], pad[1, 1, r, c]
    even, odd = yield from to_far(ur * o1r - ui * o1i, ur * o1i + ui * o1r, tab)
    hi, lo = split(meas[a, b])
    m = dot(hi, tab[PERM]) + dot(lo, tab[PERM])
    order[0], order[1] = m[:, :HALF], m[:, HALF:]

    def pull(f, start):
        pick = pl.ds(start, HALF, stride=2)
        m = jnp.concatenate([order[0, pick, :], order[1, pick, :]], axis=1)
        fr, fi = f[:HALF], f[HALF:]
        d = (fr * fr + fi * fi - m) * (2.0 * weight)
        return jnp.concatenate([d * fr, -(d * fi)], axis=0)

    gr, gi = yield from from_far(pull(even, 0), pull(odd, 1), tab)
    grad[1, 0, r, c] += ur * gr - ui * gi
    grad[1, 1, r, c] -= ur * gi + ui * gr
    o1r, o1i = pad[1, 0, r, c], pad[1, 1, r, c]
    gr, gi = yield from spread(o1r * gr - o1i * gi, o1r * gi + o1i * gr, tab)
    pr, pi = probe[0], probe[1]
    grad[0, 0, r, c] += pr * gr - pi * gi
    grad[0, 1, r, c] -= pr * gi + pi * gr
    o0r, o0i = pad[0, 0, r, c], pad[0, 1, r, c]
    pgrad[0:SIDE] += o0r * gr - o0i * gi
    pgrad[SIDE:] -= o0r * gi + o0i * gr


def run(work):
    work = list(work)
    while work:
        for w in list(work):
            if next(w, work) is work:
                work.remove(w)


MESH = pl.DeviceIdType.MESH


def kernel(tiles, pats, scanned_in, obj, meas_in, probe_in, tab_in, out_obj, out_probe,
           scanned, pad, grad, meas, probe, tab, order, pgrad, from_left, from_up, half, part, total,
           local_sem, halo_send, halo_recv, grad_send, grad_recv, sum_send, sum_recv, inside):
    tile, pat = lax.axis_index("tile"), lax.axis_index("pat")
    left, right = {"pat": lax.rem(pat + pats - 1, pats)}, {"pat": lax.rem(pat + 1, pats)}
    up, down = {"tile": lax.rem(tile + tiles - 1, tiles)}, {"tile": lax.rem(tile + 1, tiles)}

    def remote(src, dst, send, recv, k, device):
        return pltpu.make_async_remote_copy(
            src_ref=src, dst_ref=dst, send_sem=send.at[k], recv_sem=recv.at[k],
            device_id=device, device_id_type=MESH)

    loads = [
        pltpu.make_async_copy(obj, pad.at[:, :, pl.ds(0, 512), pl.ds(0, 256)], local_sem.at[0]),
        pltpu.make_async_copy(probe_in, probe, local_sem.at[1]),
        pltpu.make_async_copy(tab_in, tab, local_sem.at[2]),
        pltpu.make_async_copy(meas_in, meas, local_sem.at[3]),
        pltpu.make_async_copy(scanned_in, scanned, local_sem.at[9]),
    ]
    barrier = pltpu.get_barrier_semaphore()
    side_x, side_y = pat // 4, lax.rem(pat, 4)
    along_x = [{"pat": lax.rem(side_x + n, 4) * 4 + side_y} for n in (1, 2, 3)]
    along_y = [{"pat": side_x * 4 + lax.rem(side_y + n, 4)} for n in (1, 2, 3)]
    along_tile = [{"tile": lax.rem(tile + o, tiles)} for o in (1, tiles - 1, 2, 3, 4, 5, 6)]
    for device in [left, right] + along_y + along_x + along_tile:
        pl.semaphore_signal(barrier, inc=1, device_id=device, device_id_type=MESH)
    pl.semaphore_wait(barrier, tiles - 1 + 8)

    first, second = pl.ds(0, HALF), pl.ds(256, HALF)
    chunk = [pl.ds(k * HALF, HALF) for k in range(5)]
    piece = [pl.ds(k * 64, 64) for k in range(8)]
    beside = [
        remote(obj.at[:, :, piece[k], first], pad.at[:, :, piece[k], second], halo_send, halo_recv, k, left)
        for k in range(8)
    ]
    below = remote(obj.at[:, :, chunk[0], :], pad.at[:, :, chunk[4], pl.ds(0, 256)], halo_send, halo_recv, 8, up)
    corner = remote(pad.at[:, :, chunk[0], second], pad.at[:, :, chunk[4], second], halo_send, halo_recv, 9, up)
    core = lax.rem(tile, 2)

    @pl.when(core == 0)
    def _():
        for k in range(8):
            beside[k].start()

    below.start()
    for copy in loads:
        copy.start()
    grad[...] = jnp.zeros_like(grad)
    pgrad[...] = jnp.zeros_like(pgrad)
    for copy in loads:
        copy.wait()

    low_first = remote(
        grad.at[:, :, chunk[4], first], from_up.at[:, :, :, first], grad_send, grad_recv, 6, down)
    low = remote(
        grad.at[:, :, chunk[4], chunk[1]], from_up.at[:, :, :, chunk[1]], grad_send, grad_recv, 4, down)
    low_corner = remote(
        grad.at[:, :, chunk[4], second], from_up.at[:, :, :, second], grad_send, grad_recv, 5, down)
    out = [
        remote(grad.at[:, :, chunk[k], second], from_left.at[:, :, chunk[k], :], grad_send, grad_recv, k, right)
        for k in range(4)
    ]

    def add_corner():
        grad[:, :, 0:HALF, 256:] += from_up[:, :, :, 256:]
        out[0].start()

    def step(i, _):
        @pl.when(i == 1)
        def _():
            below.wait()

        @pl.when(i == 2)
        def _():
            @pl.when(core == 1)
            def _():
                for k in range(3):
                    beside[k].start()

            for device in along_y:
                pl.semaphore_signal(inside.at[0], inc=1, device_id=device, device_id_type=MESH)
            low_first.start()
            for k in range(5):
                beside[k].wait_send()
                pl.when(core == 1)(beside[k + 3].start)
                if k == 2:
                    beside[0].wait_recv()
                    beside[1].wait_recv()
                    corner.start()
            for k in range(2, 6):
                beside[k].wait_recv()

        @pl.when(i == 3)
        def _():
            out[1].start()
            pl.semaphore_wait(inside.at[0], 3)
            for device in along_x:
                pl.semaphore_signal(inside.at[1], inc=1, device_id=device, device_id_type=MESH)

            @pl.when(core == 1)
            def _():
                low_corner.wait_recv()
                add_corner()

            for k in range(5, 8):
                beside[k].wait_send()
            beside[6].wait_recv()
            beside[7].wait_recv()
            corner.wait()

        b = i // 2
        a = 2 * i - 4 * b
        run(
            point(scanned, pad, grad, meas, probe, pgrad, tab, order.at[k], a + k, b)
            for k in range(2)
        )
        return 0

    lax.fori_loop(0, 4, step, 0)

    other = {"tile": tile + 1 - 2 * core}
    layer = tile // 2
    half_of = lambda c: pl.ds(pl.multiple_of(c * 256, 256), 256)
    trips = [(x, y, z) for x in range(4) for y in range(4) for z in range(4)][1:]
    trips.sort(key=lambda t: -sum(min(n, 4 - n) for n in t))

    def goal(trip):
        x, y, z = (lax.rem(v + n, 4) for v, n in zip((side_x, side_y, layer), trip))
        return (x * 4 + y) * 4 + z, {"pat": x * 4 + y, "tile": z * 2 + core}

    def cell(c):
        return (pl.ds(pl.multiple_of(core * 256 + (c // 2) * 8, 8), 8),
                pl.ds(pl.multiple_of(lax.rem(c, 2) * HALF, HALF), HALF))

    own = cell(goal((0, 0, 0))[0])
    swap = remote(pgrad.at[half_of(1 - core), :], half, sum_send, sum_recv, 0, other)
    swap.start()
    low_corner.start()

    @pl.when(core == 0)
    def _():
        out[2].start()
        out[3].start()

    pl.semaphore_wait(inside.at[1], 3)
    swap.wait_recv()
    pgrad[half_of(core), :] += half[...]
    for n, trip in enumerate(trips):
        c, device = goal(trip)
        remote(pgrad.at[cell(c)], part.at[n], sum_send, sum_recv, 1, device).start()
    low_corner.wait_send()
    low.start()
    pl.when(core == 1)(out[2].start)
    remote(part, part, sum_send, sum_recv, 1, other).wait()
    acc = pgrad[own]
    for n in range(len(trips)):
        acc = acc + part[n]
    total[own] = acc
    for trip in trips:
        remote(total.at[own], total.at[own], sum_send, sum_recv, 2, goal(trip)[1]).start()

    pl.when(core == 1)(out[3].start)

    @pl.when(core == 0)
    def _():
        low_corner.wait_recv()
        add_corner()

    def finish(k):
        out[k].wait()
        if k == 0:
            low_first.wait()
            low.wait()
            grad[:, :, 0:HALF, 0:256] += from_up[:, :, :, 0:256]
        out_obj[:, :, chunk[k], 0:HALF] = grad[:, :, chunk[k], 0:HALF] + from_left[:, :, chunk[k], :]
        out_obj[:, :, chunk[k], HALF:] = grad[:, :, chunk[k], HALF:256]

    finish(1)
    remote(part, part, sum_send, sum_recv, 2, other).wait()
    mine = half_of(core)
    back = remote(total.at[mine, :], out_probe.at[core], sum_send, sum_recv, 3, other)
    back.start()
    out_probe[core] = total[mine, :]
    finish(2)
    finish(3)
    finish(0)
    back.wait()
    swap.wait_send()


def on_device(scanned, measured, obj, probe):
    tiles, pats = lax.axis_size("tile"), lax.axis_size("pat")
    table = jnp.asarray(tables())
    anywhere = pl.BlockSpec(memory_space=pl.ANY)
    f32 = jnp.float32
    vmem = lambda *shape: pltpu.VMEM(shape, f32)
    dma = lambda n: pltpu.SemaphoreType.DMA((n,))
    grad_obj, grad_probe = pl.pallas_call(
        functools.partial(kernel, tiles, pats),
        out_shape=[pltpu.VMEM(obj.shape, f32), pltpu.VMEM(probe.shape, f32)],
        in_specs=[anywhere] * 5,
        out_specs=[pl.BlockSpec(memory_space=pltpu.VMEM)] * 2,
        scratch_shapes=[
            pltpu.VMEM(scanned.T.shape, jnp.int32), vmem(2, 2, 640, 384), vmem(2, 2, 640, 384), vmem(4, 2, SIDE, SIDE), vmem(2, SIDE, SIDE),
            pltpu.VMEM(table.shape, jnp.bfloat16), vmem(2, 2, SIDE, HALF), vmem(2 * SIDE, SIDE),
            vmem(2, 2, 512, HALF), vmem(2, 2, HALF, 384),
            vmem(SIDE, SIDE), vmem(63, 8, HALF), vmem(2 * SIDE, SIDE),
            dma(10), dma(10), dma(10), dma(7), dma(7), dma(4), dma(4), pltpu.SemaphoreType.REGULAR((2,)),
        ],
        compiler_params=pltpu.CompilerParams(
            collective_id=0, has_side_effects=True, vmem_limit_bytes=56 * 2**20),
        cost_estimate=pl.CostEstimate(flops=27 * 10**9, bytes_accessed=10 * 2**20, transcendentals=0),
    )(scanned.T, obj, measured, probe, table)
    return grad_obj, grad_probe


def solution(mesh):
    in_specs = (P("tile", "pat"), P("tile", "pat", None, None), P(None, None, "tile", "pat"), P())
    out_specs = (P(None, None, "tile", "pat"), P())
    return jax.shard_map(
        on_device, mesh=mesh, in_specs=in_specs, out_specs=out_specs, check_vma=False
    )
```
